32 devices in a mesh: dp: 2 (over core), seq: 16 (over z, y, x).
Axes of the slice: x: 2, y: 2, z: 4, core: 2. Of those that a mesh axis runs over, the one named last changes fastest.
Arguments:
- queries: bfloat16 [16384, 1024], P(('dp', 'seq')), may hold values from -20 to 20
- keys: bfloat16 [16384, 1024], P(('dp', 'seq')), may hold values from -12 to 12
- value_sel: bfloat16 [16384, 4, 2, 256], P(('dp', 'seq')), may hold values from -6 to 6
- expert_logits: float32 [16384, 4, 16], P(('dp', 'seq')), may hold values from -8 to 8
- expert_index: int32 [16384, 4, 2], P(('dp', 'seq')), may hold values from 0 to 15, all different within a row
- doc_lengths: int32 [2, 16], P('dp'), may hold values from 1 to 1536, 8192 in all within a row
- group_plan: int32 [2], replicated, may hold values from 0 to 1, each once
- grad_attended: bfloat16 [16384, 1024], P(('dp', 'seq')), may hold values from -6 to 6
Outputs:
- attended: bfloat16 [16384, 1024], P(('dp', 'seq'))
- grad_queries: bfloat16 [16384, 1024], P(('dp', 'seq'))
- grad_keys: bfloat16 [16384, 1024], P(('dp', 'seq'))
- grad_value_sel: bfloat16 [16384, 4, 2, 256], P(('dp', 'seq'))
- router_logit_gradient: float32 [16384, 4, 16], P(('dp', 'seq'))
The draws below stay inside these ranges and needn't reach their ends.
Inputs may be any that keep to these rules, and one draw needn't show every extreme that they name: `doc_lengths`: each row sums to 8192; the longest document of each pack has exactly 1536 tokens. `group_plan`: a permutation of the data groups. `expert_index`: the 2 experts of a token and head differ.
All inputs are finite; a program needn't handle non-finite values.
Results may differ from the reference program's by a relative error of at most 0.006.
Values may be sent and summed in bfloat16 or wider, within the bound.
No kernel may reach another device: no remote copies, remote signals or barrier semaphores. Data moves between devices by JAX's collectives and lax.ppermute only.
A program may use at most 128 MiB of HBM per device.

```python
import math
import jax
import jax.numpy as jnp
import numpy as np
from jax import lax

HEAD_NUMBER = 4
HEAD_WIDTH = 256
E = 16
TOP = 2
TOK_DEV = 512
PACK_TOKENS = 8192
TOKENS = 16384
NDOC = 16
N_DP = 2
N_SEQ = 16


def common_keys(key):
    drawn = jax.random.normal(jax.random.fold_in(key, 11), (TOKENS, HEAD_NUMBER * HEAD_WIDTH), jnp.float32)
    return jnp.clip(drawn, -6.0, 6.0)


def draw_keys(key, part):
    common = common_keys(key)
    return common.astype(jnp.bfloat16)


def draw_queries(key, part):
    drawn = jax.random.normal(jax.random.fold_in(key, 23), (TOKENS, HEAD_NUMBER * HEAD_WIDTH), jnp.float32)
    drawn = jnp.clip(drawn, -6.0, 6.0)
    return drawn.astype(jnp.bfloat16)


def levels(stream_key, dims, pieces, smallest, largest):
    loudness, own = 1.0, jax.random.fold_in(stream_key, 6)
    for dim, blocks in pieces:
        steps = jnp.exp(jax.random.uniform(jax.random.fold_in(own, dim), (blocks,), jnp.float32, smallest / len(pieces), largest / len(pieces)))
        loudness = loudness * jnp.repeat(steps, dims[dim] // blocks).reshape([-1 if axis == dim else 1 for axis in range(len(dims))])
    return loudness


def distinct(key, rows, number_of, top, lift):
    ranking = jax.random.permutation(jax.random.fold_in(key, 1), number_of)
    boost = ranking
    for power in range(3):
        boost = boost * boost // number_of
    boost = boost * lift // number_of
    chance = jax.random.randint(jax.random.fold_in(key, 2), (rows, number_of), 0, 4096) + boost
    fixed_rows = jax.random.permutation(jax.random.fold_in(key, 3), rows)[jnp.arange(number_of) % rows]
    chance = jnp.where(jnp.arange(rows)[:, None] == fixed_rows[None, :], 1 << 14, chance)
    merit = chance * number_of + jnp.arange(number_of)
    return lax.top_k(merit.astype(jnp.int32), top)[1].astype(jnp.int32)


def profile(amount, total, reach, lean):
    weights = [(1 << 20) // math.isqrt(standing ** lean) + 1 for standing in range(2, amount + 1)]
    surplus, counts = total - reach - (amount - 1), [1] * (amount - 1)
    while surplus > 0:
        movable = [i for i in range(amount - 1) if counts[i] < reach]
        pool, left = sum([weights[i] for i in movable]), surplus
        for i in movable:
            addition = min(reach - counts[i], max(1, left * weights[i] // pool), surplus)
            counts[i] = counts[i] + addition
            surplus = surplus - addition
    return np.array([reach] + counts)


def ragged_sizes(key, number_of, total, most, slope):
    if number_of == 2:
        one = jax.random.randint(key, (), max(1, total - most), min(most, total - 1) + 1)
        return jnp.stack([one, total - one])
    sizes = jnp.asarray(profile(number_of, total, most, slope), jnp.int32)
    twos = (number_of - 1) // 2
    donor, sink = sizes[1:1 + 2 * twos:2], sizes[2:2 + 2 * twos:2]
    margin = jnp.minimum(donor - 1, most - sink)
    shifted = jax.random.randint(jax.random.fold_in(key, 1), (twos,), 0, 1 << 20) % (margin + 1)
    sizes = sizes.at[1:1 + 2 * twos:2].set(donor - shifted).at[2:2 + 2 * twos:2].set(sink + shifted)
    return sizes[jax.random.permutation(jax.random.fold_in(key, 2), number_of)]


def centred(own_key, dims, width, limit, shards=(), kind=jnp.bfloat16):
    level = levels(own_key, dims, shards, -0.22, 0.18) if shards else 1.0
    result = jax.random.normal(own_key, dims, jnp.float32) * width * level
    return jnp.minimum(jnp.maximum(result, -limit), limit).astype(kind)


def setup_inputs(seed: int = 0) -> dict:
    arg_keys = jax.random.split(jax.random.key(seed), 9)
    queries = draw_queries(jax.random.fold_in(arg_keys[8], 71), 0)
    keys = draw_keys(jax.random.fold_in(arg_keys[8], 71), 0)
    value_sel = centred(arg_keys[2], (TOKENS, HEAD_NUMBER, TOP, HEAD_WIDTH), 1.0, 6.0, ((0, 32),))
    expert_logits = centred(arg_keys[3], (TOKENS, HEAD_NUMBER, E), 2.0, 8.0, ((0, 32),), jnp.float32)
    expert_index = distinct(arg_keys[4], TOKENS * HEAD_NUMBER, E, TOP, 2048).reshape((TOKENS, HEAD_NUMBER, TOP))
    doc_lengths = jax.vmap(lambda own: ragged_sizes(own, NDOC, PACK_TOKENS, 3 * TOK_DEV, 2))(jax.random.split(arg_keys[5], N_DP)).reshape((N_DP, NDOC)).astype(jnp.int32)
    group_plan = jax.random.permutation(arg_keys[6], N_DP).astype(jnp.int32)
    grad_attended = centred(arg_keys[7], (TOKENS, HEAD_NUMBER * HEAD_WIDTH), 1.0, 6.0, ((0, 32),))
    return {"queries": queries, "keys": keys, "value_sel": value_sel, "expert_logits": expert_logits, "expert_index": expert_index, "doc_lengths": doc_lengths, "group_plan": group_plan, "grad_attended": grad_attended}


def gate_table(expert_logits, expert_index):
    experts = expert_logits.shape[2]
    onehot = (expert_index[..., None] == jnp.arange(experts, dtype=jnp.int32)).astype(jnp.float32)
    chosen = lax.optimization_barrier(jnp.sum(onehot * expert_logits[:, :, None, :], axis=3))
    return (jax.nn.sigmoid(chosen), onehot)

def doc_index(positions, doc_ends):
    return lax.optimization_barrier(jnp.sum((doc_ends[None, :] <= positions[:, None]).astype(jnp.int32), axis=1))

def attend_block(query_blk, near_keys, near_values, grad_blk, query_pos, key_pos, doc_ends):
    scale = 1.0 / math.sqrt(query_blk.shape[2])
    allowed = doc_index(query_pos, doc_ends)[:, None] == doc_index(key_pos, doc_ends)[None, :]
    allowed = allowed & (key_pos[None, :] <= query_pos[:, None]) & (key_pos[None, :] >= 0)
    scores = jnp.einsum('qhd,khd->hqk', query_blk.astype(jnp.float32), near_keys.astype(jnp.float32)) * scale
    scores = jnp.where(allowed[None], scores, -1e+30)
    top_score = lax.optimization_barrier(jnp.max(scores, axis=2, keepdims=True))
    expo = jnp.exp(scores - top_score)
    probs = expo / lax.optimization_barrier(jnp.sum(expo, axis=2, keepdims=True))
    probs_low = probs.astype(jnp.bfloat16)
    out = jnp.einsum('hqk,khd->qhd', probs_low.astype(jnp.float32), near_values.astype(jnp.float32))
    grad_f = grad_blk.astype(jnp.float32)
    dprobs = jnp.einsum('qhd,khd->hqk', grad_f, near_values.astype(jnp.float32))
    delta = lax.optimization_barrier(jnp.sum(grad_f * out, axis=2))
    dscores = (probs * (dprobs - jnp.transpose(delta)[:, :, None]) * scale).astype(jnp.bfloat16)
    query_gradient = jnp.einsum('hqk,khd->qhd', dscores.astype(jnp.float32), near_keys.astype(jnp.float32))
    key_terms = jnp.einsum('hqk,qhd->khd', dscores.astype(jnp.float32), query_blk.astype(jnp.float32))
    value_terms = jnp.einsum('hqk,qhd->khd', probs_low.astype(jnp.float32), grad_f)
    return (out.astype(jnp.bfloat16), query_gradient.astype(jnp.bfloat16), key_terms, value_terms)

def collect(terms, blocks, rows):
    shaped = terms.reshape((blocks, 4, rows) + terms.shape[2:])
    padded = jnp.concatenate([shaped, jnp.zeros((3,) + shaped.shape[1:], jnp.float32)], axis=0)
    total = padded[3:3 + blocks, 0]
    for offset in range(1, 4):
        total = total + padded[3 - offset:3 - offset + blocks, offset]
    return total.reshape((blocks * rows,) + terms.shape[2:])

def pack_terms(queries, keys, value_sel, expert_logits, expert_index, lengths, grad_attended):
    rows = TOK_DEV
    blocks = N_SEQ
    gate_weights, onehot = gate_table(expert_logits, expert_index)
    mixed = lax.optimization_barrier(jnp.sum(gate_weights[..., None] * value_sel.astype(jnp.float32), axis=2)).astype(jnp.bfloat16)
    shaped_q = queries.reshape(PACK_TOKENS, HEAD_NUMBER, HEAD_WIDTH)
    shaped_g = grad_attended.reshape(PACK_TOKENS, HEAD_NUMBER, HEAD_WIDTH)
    lead = jnp.zeros((3 * rows, HEAD_NUMBER, HEAD_WIDTH), jnp.bfloat16)
    padded_keys = jnp.concatenate([lead, keys.reshape(PACK_TOKENS, HEAD_NUMBER, HEAD_WIDTH)], axis=0)
    padded_values = jnp.concatenate([lead, mixed], axis=0)
    doc_ends = jnp.cumsum(lengths).astype(jnp.int32)

    def one_block(block_idx):
        start = (block_idx * rows).astype(jnp.int32)
        query_blk = lax.dynamic_slice_in_dim(shaped_q, start, rows, 0)
        grad_blk = lax.dynamic_slice_in_dim(shaped_g, start, rows, 0)
        near_keys = lax.dynamic_slice_in_dim(padded_keys, start, 4 * rows, 0)
        near_values = lax.dynamic_slice_in_dim(padded_values, start, 4 * rows, 0)
        query_pos = start + jnp.arange(rows, dtype=jnp.int32)
        key_pos = start - 3 * rows + jnp.arange(4 * rows, dtype=jnp.int32)
        return attend_block(query_blk, near_keys, near_values, grad_blk, query_pos, key_pos, doc_ends)
    attended, query_gradient, key_terms, value_terms = lax.map(one_block, jnp.arange(blocks, dtype=jnp.int32))
    key_gradient = collect(key_terms, blocks, rows)
    value_sum_total = collect(value_terms, blocks, rows)
    selected_value_gradient = (gate_weights[..., None] * value_sum_total[:, :, None, :]).astype(jnp.bfloat16)
    gate_grad = lax.optimization_barrier(jnp.sum(value_sum_total[:, :, None, :] * value_sel.astype(jnp.float32), axis=3))
    chosen_grad = gate_grad * gate_weights * (1.0 - gate_weights)
    router_logit_gradient = lax.optimization_barrier(jnp.sum(onehot * chosen_grad[..., None], axis=2))
    return (attended.reshape(PACK_TOKENS, HEAD_NUMBER * HEAD_WIDTH), query_gradient.reshape(PACK_TOKENS, HEAD_NUMBER * HEAD_WIDTH), key_gradient.astype(jnp.bfloat16).reshape(PACK_TOKENS, HEAD_NUMBER * HEAD_WIDTH), selected_value_gradient, router_logit_gradient)

def reference(queries, keys, value_sel, expert_logits, expert_index, doc_lengths, group_plan, grad_attended):
    results = []
    for pack in range(N_DP):
        lo = pack * PACK_TOKENS
        hi = lo + PACK_TOKENS
        results.append(pack_terms(queries[lo:hi], keys[lo:hi], value_sel[lo:hi], expert_logits[lo:hi], expert_index[lo:hi], doc_lengths[pack], grad_attended[lo:hi]))
    inverse = jnp.argsort(group_plan).astype(jnp.int32)
    finals = []
    for member in range(5):
        stacked = jnp.stack([res[member] for res in results], axis=0)
        placed = jnp.take(stacked, inverse, axis=0)
        finals.append(placed.reshape((N_DP * PACK_TOKENS,) + stacked.shape[2:]))
    return (finals[0], finals[1], finals[2], finals[3], finals[4])
```

```python
import functools
import math

import jax
import jax.numpy as jnp
from jax import lax
from jax.experimental import pallas as pl
from jax.experimental.pallas import tpu as pltpu
from jax.sharding import PartitionSpec as P

HALO = 3
NEG = -1e30
QT = 256
KT = 256
VMEM = pltpu.VMEM
SMEM = pltpu.SMEM
LOG2E = math.log2(math.e)


def spec(space):
    return pl.BlockSpec(memory_space=space)


def params(mib=48):
    return pltpu.CompilerParams(vmem_limit_bytes=mib * 1024 * 1024)


def pick(me, x, k, width):
    return x[:, pl.ds(pl.multiple_of((me ^ k) * width, width), width)]


def pack_kernel(me_ref, x_ref, *piece_refs):
    for k, piece in enumerate(piece_refs):
        piece[...] = pick(me_ref[0], x_ref, k, piece.shape[1])


def pack(me, x, heads):
    rows, width = x.shape[0], x.shape[1] // heads
    return pl.pallas_call(
        pack_kernel,
        out_shape=[jax.ShapeDtypeStruct((rows, width), x.dtype)] * heads,
        in_specs=[spec(SMEM), spec(VMEM)],
        out_specs=[spec(VMEM)] * heads,
        compiler_params=params(),
        cost_estimate=pl.CostEstimate(flops=0, bytes_accessed=4 * x.size, transcendentals=0),
        name="pack",
    )(me, x)


def mix_kernel(heads, top, me_ref, gates_ref, values_ref, *refs):
    piece_refs, mixed = refs[:-1], refs[-1]
    width = piece_refs[0].shape[1]
    for h in range(heads):
        total = 0.0
        for j in range(top):
            col = h * top + j
            gate = gates_ref[:, col : col + 1]
            total += gate * values_ref[:, col * width : (col + 1) * width].astype(jnp.float32)
        mixed[:, h * width : (h + 1) * width] = total.astype(mixed.dtype)
    for k, piece in enumerate(piece_refs):
        piece[...] = pick(me_ref[0], mixed, k, width)


def mix(me, gates, values, heads, top):
    rows, width = values.shape[0], values.shape[1] // (heads * top)
    return pl.pallas_call(
        functools.partial(mix_kernel, heads, top),
        out_shape=[jax.ShapeDtypeStruct((rows, width), values.dtype)] * heads,
        in_specs=[spec(SMEM), spec(VMEM), spec(VMEM)],
        out_specs=[spec(VMEM)] * heads,
        scratch_shapes=[VMEM((rows, heads * width), values.dtype)],
        compiler_params=params(),
        cost_estimate=pl.CostEstimate(flops=0, bytes_accessed=3 * values.size, transcendentals=0),
        name="mix",
    )(me, gates, values)


def order_kernel(skip, me_ref, *refs):
    pieces, (whole, part) = refs[:-2], refs[-2:]
    rows = pieces[0].shape[0]
    for k, piece in enumerate(pieces):
        place = me_ref[0] ^ k
        value = piece[...]
        whole[pl.ds(pl.multiple_of(place * rows, rows), rows), :] = value
        kept = place - skip

        @pl.when((kept >= 0) & (kept < part.shape[0] // rows))
        def _():
            part[pl.ds(pl.multiple_of(kept * rows, rows), rows), :] = value


def order(me, pieces, skip):
    rows, width = pieces[0].shape
    return pl.pallas_call(
        functools.partial(order_kernel, skip),
        out_shape=[
            jax.ShapeDtypeStruct((len(pieces) * rows, width), pieces[0].dtype),
            jax.ShapeDtypeStruct((HALO * rows, width), pieces[0].dtype),
        ],
        in_specs=[spec(SMEM)] + [spec(VMEM)] * len(pieces),
        out_specs=[spec(VMEM)] * 2,
        compiler_params=params(),
        cost_estimate=pl.CostEstimate(
            flops=0, bytes_accessed=12 * rows * width, transcendentals=0
        ),
        name="order",
    )(me, *pieces)


def first_key(position, ends_ref):
    found = jnp.zeros_like(position)
    for n in range(ends_ref.shape[0]):
        found = jnp.where(ends_ref[n] <= position, ends_ref[n], found)
    return found


def dot_nt(a, b):
    return lax.dot_general(a, b, (((1,), (1,)), ((), ())), preferred_element_type=jnp.float32)


def dot_nn(a, b):
    return lax.dot_general(a, b, (((1,), (0,)), ((), ())), preferred_element_type=jnp.float32)


def lanes(start, size):
    return pl.ds(pl.multiple_of(start, size), size)


def transposed(x):
    return x.T


def fill(dst, parts):
    at = 0
    for part in parts:
        dst[at : at + part.shape[0], :] = part[...]
        at += part.shape[0]


def fill_transposed(dst, parts):
    at = 0
    for part in parts:
        for lo in range(0, part.shape[0], KT):
            dst[:, at + lo : at + lo + KT] = transposed(part[lo : lo + KT, :])
        at += part.shape[0]


def query_tile(base, lo, ends_ref, origin):
    pos = base + lo + lax.broadcasted_iota(jnp.int32, (1, QT), 1)
    start = jnp.zeros((), jnp.int32) + base + lo
    return pos - origin, first_key(pos, ends_ref) - origin, first_key(start, ends_ref) - origin


def allowed(key_lo, query_row, first_row):
    key = lax.broadcasted_iota(jnp.int32, (KT, QT), 0)
    return (key >= first_row - key_lo) & (key <= query_row - key_lo)


def forward_kernel(
    scale, meta_ref, ends_ref, kh, kf, vh, vf, q_ref, g_ref, *refs
):
    piece_refs = refs[:-4]
    stats, k_all, v_t, out_all = refs[-4:]
    me, base = meta_ref[0], meta_ref[1]
    width = q_ref.shape[1]
    halo_rows = kh.shape[0]
    origin = base - halo_rows
    fill(k_all, (kh, kf))
    fill_transposed(v_t, (vh, vf))

    def one_tile(i, carry):
        lo = i * QT
        query_row, first_row, first = query_tile(base, lo, ends_ref, origin)
        rows = lanes(lo, QT)
        query = q_ref[rows, :]

        def step(t, state):
            top, total, acc = state
            at = lanes(t * KT, KT)
            scores = dot_nt(k_all[at, :], query) * (scale * LOG2E)
            scores = jnp.where(allowed(t * KT, query_row, first_row), scores, NEG)
            new_top = jnp.maximum(top, jnp.max(scores, axis=0, keepdims=True))
            expo = jnp.exp2(scores - new_top)
            fade = jnp.exp2(top - new_top)
            total = total * fade + jnp.sum(expo, axis=0, keepdims=True)
            acc = acc * fade + dot_nn(v_t[:, at], expo.astype(jnp.bfloat16))
            return new_top, total, acc

        state = (
            jnp.full((1, QT), NEG, jnp.float32),
            jnp.zeros((1, QT), jnp.float32),
            jnp.zeros((width, QT), jnp.float32),
        )
        last = (halo_rows + lo + QT - 1) // KT + 1
        top, total, acc = lax.fori_loop(first // KT, last, step, state)
        out = transposed(acc / total)
        out_all[rows, :] = out.astype(out_all.dtype)
        stats[0:1, rows] = top + jnp.log2(total)
        product = g_ref[rows, :].astype(jnp.float32) * out
        stats[1:2, rows] = jnp.sum(transposed(product), axis=0, keepdims=True)
        return carry

    lax.fori_loop(0, q_ref.shape[0] // QT, one_tile, 0)
    rows = piece_refs[0].shape[0]
    for k, piece in enumerate(piece_refs):
        piece[...] = out_all[lanes((me ^ k) * rows, rows), :]


def forward(meta, ends, kh, kf, vh, vf, q, g, rows):
    total, width = q.shape
    pieces = total // rows
    keys = kh.shape[0] + kf.shape[0]
    return pl.pallas_call(
        functools.partial(forward_kernel, 1.0 / math.sqrt(width)),
        out_shape=[jax.ShapeDtypeStruct((rows, width), q.dtype)] * pieces
        + [jax.ShapeDtypeStruct((2, total), jnp.float32)],
        in_specs=[spec(SMEM)] * 2 + [spec(VMEM)] * 6,
        out_specs=[spec(VMEM)] * (pieces + 1),
        scratch_shapes=[
            VMEM((keys, width), q.dtype),
            VMEM((width, keys), q.dtype),
            VMEM((total, width), q.dtype),
        ],
        compiler_params=params(),
        cost_estimate=pl.CostEstimate(
            flops=4 * total * keys * width // 4, bytes_accessed=16 * total * width, transcendentals=0
        ),
        name="forward",
    )(meta, ends, kh, kf, vh, vf, q, g)


def tile_terms(scale, key, value, query, grad, lse, delta, mask):
    scores = dot_nt(key, query) * (scale * LOG2E) - lse
    probs = jnp.exp2(jnp.where(mask, scores, NEG))
    dprobs = dot_nt(value, grad)
    return probs.astype(jnp.bfloat16), (probs * (dprobs - delta)).astype(jnp.bfloat16)


def backward_kernel(scale, meta_ref, ends_ref, kh, kf, vh, vf, q_ref, g_ref, stats, *refs):
    piece_refs = refs[:-6]
    dk_ref, dv_ref, k_all, v_all, k_t, dq_all = refs[-6:]
    me, base = meta_ref[0], meta_ref[1]
    width = q_ref.shape[1]
    halo_rows = kh.shape[0]
    origin = base - halo_rows
    fill(k_all, (kh, kf))
    fill(v_all, (vh, vf))
    fill_transposed(k_t, (kh, kf))
    dk_ref[...] = jnp.zeros_like(dk_ref)
    dv_ref[...] = jnp.zeros_like(dv_ref)

    def one_tile(i, carry):
        lo = i * QT
        query_row, first_row, first = query_tile(base, lo, ends_ref, origin)
        rows = lanes(lo, QT)
        query, grad = q_ref[rows, :], g_ref[rows, :]
        lse, delta = stats[0:1, rows], stats[1:2, rows]

        def step(own, t, acc):
            at = lanes(t * KT, KT)
            mask = allowed(t * KT, query_row, first_row)
            probs, dscores = tile_terms(
                scale, k_all[at, :], v_all[at, :], query, grad, lse, delta, mask
            )
            if own:
                here = lanes(t * KT - halo_rows, KT)
                dv_ref[here, :] += dot_nn(probs, grad)
                dk_ref[here, :] += dot_nn(dscores, query)
            return acc + dot_nn(k_t[:, at], dscores)

        acc = jnp.zeros((width, QT), jnp.float32)
        split = halo_rows // KT
        last = (halo_rows + lo + QT - 1) // KT + 1
        acc = lax.fori_loop(first // KT, split, functools.partial(step, False), acc)
        acc = lax.fori_loop(
            jnp.maximum(first // KT, split), last, functools.partial(step, True), acc
        )
        dq_all[rows, :] = transposed(acc * scale).astype(dq_all.dtype)
        return carry

    lax.fori_loop(0, q_ref.shape[0] // QT, one_tile, 0)
    rows = piece_refs[0].shape[0]
    for k, piece in enumerate(piece_refs):
        piece[...] = dq_all[lanes((me ^ k) * rows, rows), :]


def backward(meta, ends, kh, kf, vh, vf, q, g, stats, rows):
    total, width = q.shape
    pieces = total // rows
    keys = kh.shape[0] + kf.shape[0]
    return pl.pallas_call(
        functools.partial(backward_kernel, 1.0 / math.sqrt(width)),
        out_shape=[jax.ShapeDtypeStruct((rows, width), q.dtype)] * pieces
        + [jax.ShapeDtypeStruct((total, width), jnp.float32)] * 2,
        in_specs=[spec(SMEM)] * 2 + [spec(VMEM)] * 7,
        out_specs=[spec(VMEM)] * (pieces + 2),
        scratch_shapes=[
            VMEM((keys, width), q.dtype),
            VMEM((keys, width), q.dtype),
            VMEM((width, keys), q.dtype),
            VMEM((total, width), q.dtype),
        ],
        compiler_params=params(),
        cost_estimate=pl.CostEstimate(
            flops=10 * total * keys * width // 4, bytes_accessed=24 * total * width, transcendentals=0
        ),
        name="backward",
    )(meta, ends, kh, kf, vh, vf, q, g, stats)


def later_kernel(scale, meta_ref, ends_ref, kf, vf, qh, gh, stats, dk_in, dv_in, *refs):
    half = (len(refs) - 2) // 2
    dk_refs, dv_refs, (dk, dv) = refs[:half], refs[half : 2 * half], refs[2 * half :]
    me, base, limit = meta_ref[0], meta_ref[1], meta_ref[2]
    own_rows = kf.shape[0]
    dk[...] = dk_in[...]
    dv[...] = dv_in[...]

    def one_tile(i, carry):
        lo = i * QT
        query_row, first_row, first = query_tile(base + own_rows, lo, ends_ref, base)
        rows = lanes(lo, QT)
        query, grad = qh[rows, :], gh[rows, :]
        lse, delta = stats[0:1, rows], stats[1:2, rows]

        def step(t, carry):
            at = lanes(t * KT, KT)
            mask = allowed(t * KT, query_row, first_row)
            probs, dscores = tile_terms(
                scale, kf[at, :], vf[at, :], query, grad, lse, delta, mask
            )
            dv[at, :] += dot_nn(probs, grad)
            dk[at, :] += dot_nn(dscores, query)
            return carry

        return lax.fori_loop(jnp.minimum(first, own_rows) // KT, own_rows // KT, step, carry)

    tiles = jnp.where(base + own_rows < limit, qh.shape[0] // QT, 0)
    lax.fori_loop(0, tiles, one_tile, 0)
    rows = dk_refs[0].shape[0]
    for k in range(half):
        at = lanes((me ^ k) * rows, rows)
        dk_refs[k][...] = (dk[at, :] * scale).astype(dk_refs[k].dtype)
        dv_refs[k][...] = dv[at, :].astype(dv_refs[k].dtype)


def later(meta, ends, kf, vf, qh, gh, stats, dk, dv, rows):
    total, width = kf.shape
    pieces = total // rows
    return pl.pallas_call(
        functools.partial(later_kernel, 1.0 / math.sqrt(width)),
        out_shape=[jax.ShapeDtypeStruct((rows, width), kf.dtype)] * (2 * pieces),
        in_specs=[spec(SMEM)] * 2 + [spec(VMEM)] * 7,
        out_specs=[spec(VMEM)] * (2 * pieces),
        scratch_shapes=[VMEM((total, width), jnp.float32)] * 2,
        compiler_params=params(),
        cost_estimate=pl.CostEstimate(
            flops=8 * total * qh.shape[0] * width // 4,
            bytes_accessed=24 * total * width,
            transcendentals=0,
        ),
        name="later",
    )(meta, ends, kf, vf, qh, gh, stats, dk, dv)


def place_kernel(me_ref, *refs):
    pieces, whole = refs[:-1], refs[-1]
    for k, piece in enumerate(pieces):
        width = piece.shape[1]
        whole[:, lanes((me_ref[0] ^ k) * width, width)] = piece[...]


def place(me, pieces):
    rows, width = pieces[0].shape
    return pl.pallas_call(
        place_kernel,
        out_shape=jax.ShapeDtypeStruct((rows, len(pieces) * width), pieces[0].dtype),
        in_specs=[spec(SMEM)] + [spec(VMEM)] * len(pieces),
        out_specs=spec(VMEM),
        compiler_params=params(),
        cost_estimate=pl.CostEstimate(
            flops=0, bytes_accessed=16 * rows * width, transcendentals=0
        ),
        name="place",
    )(me, *pieces)


def gate_table(expert_logits, expert_index):
    experts = expert_logits.shape[2]
    onehot = (expert_index[..., None] == jnp.arange(experts, dtype=jnp.int32)).astype(jnp.float32)
    chosen = jnp.sum(onehot * expert_logits[:, :, None, :], axis=3)
    return (jax.nn.sigmoid(chosen), onehot)


def run(swap, queries, keys, value_sel, expert_logits, expert_index, doc_lengths, grad_attended):
    rows = queries.shape[0]
    heads, top, width = value_sel.shape[1:]
    blocks = lax.axis_size("seq")
    groups = lax.axis_size("dp")
    block = lax.axis_index("seq")
    me = lax.rem(block, heads)
    base = (block - me) * rows
    meta = jnp.stack([me, base, blocks * rows]).astype(jnp.int32)
    ends = jnp.cumsum(doc_lengths[0]).astype(jnp.int32)

    def partner(i, k):
        return i - i % heads + (i % heads ^ k)

    def send(x, k):
        return lax.ppermute(x, "seq", [(i, partner(i, k)) for i in range(blocks)])

    def send_back(x, k):
        if not swap:
            return send(x, k) if k else x
        route = [
            (g * blocks + i, (groups - 1 - g) * blocks + partner(i, k))
            for g in range(groups)
            for i in range(blocks)
        ]
        return lax.ppermute(x, ("dp", "seq"), route)

    def exchange(pieces):
        return [pieces[0]] + [send(pieces[k], k) for k in range(1, heads)]

    def shift(x, by):
        route = [(i, i + by) for i in range(blocks) if 0 <= i + by < blocks]
        return lax.ppermute(x, "seq", route)

    key_pieces = exchange(pack(meta, keys, heads))
    gates, onehot = gate_table(expert_logits, expert_index)
    flat_values = value_sel.reshape(rows, heads * top * width)
    value_pieces = exchange(mix(meta, gates.reshape(rows, heads * top), flat_values, heads, top))
    query_pieces = exchange(pack(meta, queries, heads))
    grad_pieces = exchange(pack(meta, grad_attended, heads))
    kf, k_up = order(meta, key_pieces, heads - HALO)
    kh = shift(k_up, heads)
    vf, v_up = order(meta, value_pieces, heads - HALO)
    vh = shift(v_up, heads)
    qf, q_down = order(meta, query_pieces, 0)
    qh = shift(q_down, -heads)
    gf, g_down = order(meta, grad_pieces, 0)
    gh = shift(g_down, -heads)

    *out_pieces, stats = forward(meta, ends, kh, kf, vh, vf, qf, gf, rows)
    out_got = [send_back(x, k) for k, x in enumerate(out_pieces)]
    later_stats = shift(stats[:, : HALO * rows], -heads)
    *dq_pieces, dk, dv = backward(meta, ends, kh, kf, vh, vf, qf, gf, stats, rows)
    dq_got = [send_back(x, k) for k, x in enumerate(dq_pieces)]
    pieces = later(meta, ends, kf, vf, qh, gh, later_stats, dk, dv, rows)
    dk_got = [send_back(x, k) for k, x in enumerate(pieces[:heads])]
    dv_got = [send_back(x, k) for k, x in enumerate(pieces[heads:])]

    if swap:
        other = [(g, groups - 1 - g) for g in range(groups)]
        value_sel = lax.ppermute(value_sel, "dp", other)
        expert_logits = lax.ppermute(expert_logits, "dp", other)
        expert_index = lax.ppermute(expert_index, "dp", other)
        gates, onehot = gate_table(expert_logits, expert_index)
    grad_mixed = place(meta, dv_got).reshape(rows, heads, 1, width).astype(jnp.float32)
    grad_value_sel = (gates[..., None] * grad_mixed).astype(jnp.bfloat16)
    gate_grad = jnp.sum(grad_mixed * value_sel.astype(jnp.float32), axis=3)
    chosen_grad = gate_grad * gates * (1.0 - gates)
    router_logit_gradient = jnp.sum(onehot * chosen_grad[..., None], axis=2)
    return (
        place(meta, out_got),
        place(meta, dq_got),
        place(meta, dk_got),
        grad_value_sel,
        router_logit_gradient,
    )


def shards(
    queries, keys, value_sel, expert_logits, expert_index, doc_lengths, group_plan, grad_attended
):
    operands = (
        queries,
        keys,
        value_sel,
        expert_logits,
        expert_index,
        doc_lengths,
        grad_attended,
    )
    return lax.cond(
        group_plan[0] == 0,
        functools.partial(run, False),
        functools.partial(run, True),
        *operands,
    )


def solution(mesh):
    in_specs = (
        P(("dp", "seq"), None),
        P(("dp", "seq"), None),
        P(("dp", "seq"), None, None, None),
        P(("dp", "seq"), None, None),
        P(("dp", "seq"), None, None),
        P("dp", None),
        P(),
        P(("dp", "seq"), None),
    )
    out_specs = (
        P(("dp", "seq"), None),
        P(("dp", "seq"), None),
        P(("dp", "seq"), None),
        P(("dp", "seq"), None, None, None),
        P(("dp", "seq"), None, None),
    )
    return jax.shard_map(shards, mesh=mesh, in_specs=in_specs, out_specs=out_specs, check_vma=False)
```

```python
import functools
import math

import jax
import jax.numpy as jnp
from jax import lax
from jax.experimental import pallas as pl
from jax.experimental.pallas import tpu as pltpu
from jax.sharding import PartitionSpec as P

HALO = 3
NEG = -1e30
QT = 512
KT = 512
VMEM = pltpu.VMEM
SMEM = pltpu.SMEM
LOG2E = math.log2(math.e)
STEP = 64
STAT_ROWS = 16
STAT_COLS = 256


def COST(flops, size):
    return pl.CostEstimate(flops=0, bytes_accessed=1, transcendentals=0)


def spec(space):
    return pl.BlockSpec(memory_space=space)


def params(mib=48):
    return pltpu.CompilerParams(vmem_limit_bytes=mib * 1024 * 1024)


def pick(me, x, k, width):
    return x[:, pl.ds(pl.multiple_of((me ^ k) * width, width), width)]


def pack_kernel(waits, me_ref, x_ref, *refs):
    for k, piece in enumerate(refs[waits:]):
        piece[...] = pick(me_ref[0], x_ref, k, piece.shape[1])


def pack(me, x, heads, *wait):
    rows, width = x.shape[0], x.shape[1] // heads
    return pl.pallas_call(
        functools.partial(pack_kernel, len(wait)),
        out_shape=[jax.ShapeDtypeStruct((rows, width), x.dtype)] * heads,
        in_specs=[spec(SMEM), spec(VMEM)] + [spec(pl.ANY)] * len(wait),
        out_specs=[spec(VMEM)] * heads,
        compiler_params=params(),
        cost_estimate=COST(0, 4 * x.size),
        name="pack",
    )(me, x, *wait)


def mix_kernel(waits, me_ref, gates_ref, values_ref, *refs):
    piece_refs, (mixed, columns) = refs[waits:-2], refs[-2:]
    _, heads, top, width = values_ref.shape
    columns[...] = gates_ref[...].T

    def step(i, carry):
        at = lanes(i * STEP, STEP)
        for h in range(heads):
            total = 0.0
            for j in range(top):
                col = h * top + j
                gate = columns[at, col : col + 1]
                total += gate * values_ref[at, h, j, :].astype(jnp.float32)
            mixed[at, h * width : (h + 1) * width] = total.astype(mixed.dtype)
        return carry

    lax.fori_loop(0, mixed.shape[0] // STEP, step, 0)
    for k, piece in enumerate(piece_refs):
        piece[...] = pick(me_ref[0], mixed, k, width)


def mix(me, gates, values, *wait):
    rows, heads, _, width = values.shape
    return pl.pallas_call(
        functools.partial(mix_kernel, len(wait)),
        out_shape=[jax.ShapeDtypeStruct((rows, width), values.dtype)] * heads,
        in_specs=[spec(SMEM)] + [spec(VMEM)] * 2 + [spec(pl.ANY)] * len(wait),
        out_specs=[spec(VMEM)] * heads,
        scratch_shapes=[
            VMEM((rows, heads * width), values.dtype),
            VMEM(gates.shape[::-1], jnp.float32),
        ],
        compiler_params=params(),
        cost_estimate=COST(0, 3 * values.size),
        name="mix",
    )(me, gates, values, *wait)


def order_kernel(skips, count, waits, me_ref, *refs):
    pieces, outs = refs[:count], list(refs[count + waits :])
    rows = pieces[0].shape[0] // len(skips)
    for n, skip in enumerate(skips):
        whole = outs.pop(0)
        part = None if skip is None else outs.pop(0)
        for k, piece in enumerate(pieces):
            place = me_ref[0] ^ k
            value = piece[n * rows : (n + 1) * rows, :]
            whole[lanes(place * rows, rows), :] = value
            if part is None:
                continue
            kept = place - skip

            @pl.when((kept >= 0) & (kept < part.shape[0] // rows))
            def _(part=part, kept=kept, value=value):
                part[lanes(kept * rows, rows), :] = value


def order(me, pieces, skips, *wait):
    rows, width = pieces[0].shape[0] // len(skips), pieces[0].shape[1]
    shapes = []
    for skip in skips:
        shapes.append((len(pieces) * rows, width))
        if skip is not None:
            shapes.append((HALO * rows, width))
    return pl.pallas_call(
        functools.partial(order_kernel, skips, len(pieces), len(wait)),
        out_shape=[jax.ShapeDtypeStruct(shape, pieces[0].dtype) for shape in shapes],
        in_specs=[spec(SMEM)] + [spec(VMEM)] * len(pieces) + [spec(pl.ANY)] * len(wait),
        out_specs=[spec(VMEM)] * len(shapes),
        compiler_params=params(),
        cost_estimate=COST(0, 12 * rows * width),
        name="order",
    )(me, *pieces, *wait)


def first_key(position, ends_ref):
    found = jnp.zeros_like(position)
    for n in range(ends_ref.shape[0]):
        found = jnp.where(ends_ref[n] <= position, ends_ref[n], found)
    return found


def dot_nt(a, b):
    return lax.dot_general(a, b, (((1,), (1,)), ((), ())), preferred_element_type=jnp.float32)


def dot_nn(a, b):
    return lax.dot_general(a, b, (((1,), (0,)), ((), ())), preferred_element_type=jnp.float32)


def lanes(start, size):
    return pl.ds(pl.multiple_of(start, size), size)


def transposed(x):
    return x.T


def fill_transposed(dst, src):
    def step(i, carry):
        at = lanes(i * KT, KT)
        dst[:, at] = transposed(src[at, :])
        return carry

    lax.fori_loop(0, src.shape[0] // KT, step, 0)


def query_tile(base, lo, ends_ref, origin):
    pos = base + lo + lax.broadcasted_iota(jnp.int32, (1, QT), 1)
    start = jnp.zeros((), jnp.int32) + base + lo
    return pos - origin, first_key(pos, ends_ref) - origin, first_key(start, ends_ref) - origin


def allowed(key_lo, query_row, first_row):
    key = lax.broadcasted_iota(jnp.int32, (KT, QT), 0)
    return (key >= first_row - key_lo) & (key <= query_row - key_lo)


def online_step(scale, key, value_t, query, mask, state):
    top, total, acc = state
    scores = jnp.where(mask, dot_nt(key, query) * (scale * LOG2E), NEG)
    new_top = jnp.maximum(top, jnp.max(scores, axis=0, keepdims=True))
    expo = jnp.exp2(scores - new_top)
    fade = jnp.exp2(top - new_top)
    total = total * fade + jnp.sum(expo, axis=0, keepdims=True)
    acc = acc * fade + dot_nn(value_t, expo.astype(jnp.bfloat16))
    return new_top, total, acc


def near_kernel(scale, meta_ref, ends_ref, kf, vf, q_ref, wait, out_ref, lse_ref, k_t, v_t):
    del wait
    base = meta_ref[1]
    width = q_ref.shape[1]
    fill_transposed(v_t, vf)
    fill_transposed(k_t, kf)

    def one_tile(i, carry):
        lo = i * QT
        query_row, first_row, first = query_tile(base, lo, ends_ref, base)
        rows = lanes(lo, QT)
        query = q_ref[rows, :]

        def step(t, state):
            at = lanes(t * KT, KT)
            mask = allowed(t * KT, query_row, first_row)
            return online_step(scale, kf[at, :], v_t[:, at], query, mask, state)

        state = (
            jnp.full((1, QT), NEG, jnp.float32),
            jnp.zeros((1, QT), jnp.float32),
            jnp.zeros((width, QT), jnp.float32),
        )
        last = (lo + QT - 1) // KT + 1
        top, total, acc = lax.fori_loop(jnp.maximum(first, 0) // KT, last, step, state)
        out_ref[rows, :] = transposed(acc / total)
        lse_ref[0:1, rows] = top + jnp.log2(total)
        return carry

    lax.fori_loop(0, q_ref.shape[0] // QT, one_tile, 0)


def near(meta, ends, kf, vf, q, wait):
    total, width = q.shape
    return pl.pallas_call(
        functools.partial(near_kernel, 1.0 / math.sqrt(width)),
        out_shape=[
            jax.ShapeDtypeStruct((total, width), jnp.float32),
            jax.ShapeDtypeStruct((1, total), jnp.float32),
            jax.ShapeDtypeStruct((width, total), kf.dtype),
        ],
        in_specs=[spec(SMEM)] * 2 + [spec(VMEM)] * 3 + [spec(pl.ANY)],
        out_specs=[spec(VMEM)] * 3,
        scratch_shapes=[VMEM((width, total), q.dtype)],
        compiler_params=params(),
        cost_estimate=COST(0, 4 << 20),
        name="near",
    )(meta, ends, kf, vf, q, wait)


def reach_kernel(
    scale, meta_ref, ends_ref, kh, vh, q_ref, g_ref, near_ref, near_lse, *refs
):
    piece_refs, (stats, down, out_all) = refs[:-3], refs[-3:]
    me, base = meta_ref[0], meta_ref[1]
    halo_rows = kh.shape[0]
    origin = base - halo_rows

    def one_tile(i, carry):
        lo = i * QT
        query_row, first_row, first = query_tile(base, lo, ends_ref, origin)
        rows = lanes(lo, QT)

        @pl.when(first >= halo_rows)
        def _():
            out_all[rows, :] = near_ref[rows, :]
            stats[0:1, rows] = near_lse[0:1, rows]

        @pl.when(first < halo_rows)
        def _():
            query = q_ref[rows, :]

            def step(t, state):
                at = lanes(t * KT, KT)
                mask = allowed(t * KT, query_row, first_row)
                return online_step(
                    scale, kh[at, :], transposed(vh[at, :]), query, mask, state
                )

            state = (
                near_lse[0:1, rows],
                jnp.ones((1, QT), jnp.float32),
                transposed(near_ref[rows, :]),
            )
            top, total, acc = lax.fori_loop(first // KT, halo_rows // KT, step, state)
            out_all[rows, :] = transposed(acc / total)
            stats[0:1, rows] = top + jnp.log2(total)

        product = g_ref[rows, :].astype(jnp.float32) * out_all[rows, :]
        stats[1:2, rows] = jnp.sum(transposed(product), axis=0, keepdims=True)
        return carry

    lax.fori_loop(0, q_ref.shape[0] // QT, one_tile, 0)
    rows = piece_refs[0].shape[0]
    for k, piece in enumerate(piece_refs):
        piece[...] = out_all[lanes((me ^ k) * rows, rows), :].astype(piece.dtype)
    down[:halo_rows, :] = g_ref[:halo_rows, :]
    for n in range(halo_rows // STAT_COLS):
        block = []
        for row in range(2):
            left = stats[row : row + 1, n * STAT_COLS : (n + 1) * STAT_COLS]
            for _ in range(3):
                part = left.astype(down.dtype).astype(jnp.float32)
                block.append(part)
                left = left - part
        block.append(jnp.zeros((STAT_ROWS - len(block), STAT_COLS), jnp.float32))
        lo = halo_rows + n * STAT_ROWS
        down[lo : lo + STAT_ROWS, :] = jnp.concatenate(block, axis=0).astype(down.dtype)


def reach(meta, ends, kh, vh, q, g, near_out, near_lse, rows):
    total, width = q.shape
    pieces = total // rows
    down = HALO * rows + HALO * rows // STAT_COLS * STAT_ROWS
    return pl.pallas_call(
        functools.partial(reach_kernel, 1.0 / math.sqrt(width)),
        out_shape=[jax.ShapeDtypeStruct((rows, width), q.dtype)] * pieces
        + [jax.ShapeDtypeStruct((2, total), jnp.float32), jax.ShapeDtypeStruct((down, width), g.dtype)],
        in_specs=[spec(SMEM)] * 2 + [spec(VMEM)] * 6,
        out_specs=[spec(VMEM)] * (pieces + 2),
        scratch_shapes=[VMEM((total, width), jnp.float32)],
        compiler_params=params(),
        cost_estimate=COST(0, 4 << 20),
        name="reach",
    )(meta, ends, kh, vh, q, g, near_out, near_lse)


def tile_terms(scale, key, value, query, grad, lse, delta, mask):
    scores = dot_nt(key, query) * (scale * LOG2E) - lse
    probs = jnp.exp2(jnp.where(mask, scores, NEG))
    dprobs = dot_nt(value, grad)
    return probs.astype(jnp.bfloat16), (probs * (dprobs - delta)).astype(jnp.bfloat16)


def backward_kernel(
    scale, waits, meta_ref, ends_ref, kh, kf, k_t, vh, vf, q_ref, g_ref, stats, *refs
):
    piece_refs = refs[waits:-3]
    dk_ref, dv_ref, dq_all = refs[-3:]
    me, base = meta_ref[0], meta_ref[1]
    width = q_ref.shape[1]
    halo_rows = kh.shape[0]
    origin = base - halo_rows
    dk_ref[...] = jnp.zeros_like(dk_ref)
    dv_ref[...] = jnp.zeros_like(dv_ref)

    def one_tile(i, carry):
        lo = i * QT
        query_row, first_row, first = query_tile(base, lo, ends_ref, origin)
        rows = lanes(lo, QT)
        query, grad = q_ref[rows, :], g_ref[rows, :]
        lse, delta = stats[0:1, rows], stats[1:2, rows]

        def far(t, acc):
            at = lanes(t * KT, KT)
            mask = allowed(t * KT, query_row, first_row)
            key = kh[at, :]
            _, dscores = tile_terms(scale, key, vh[at, :], query, grad, lse, delta, mask)
            return acc + dot_nn(transposed(key), dscores)

        def own(t, acc):
            at = lanes(t * KT, KT)
            mask = allowed(t * KT + halo_rows, query_row, first_row)
            probs, dscores = tile_terms(
                scale, kf[at, :], vf[at, :], query, grad, lse, delta, mask
            )
            dv_ref[at, :] += dot_nn(probs, grad)
            dk_ref[at, :] += dot_nn(dscores, query)
            return acc + dot_nn(k_t[:, at], dscores)

        acc = jnp.zeros((width, QT), jnp.float32)
        acc = lax.fori_loop(first // KT, halo_rows // KT, far, acc)
        start = jnp.maximum(first - halo_rows, 0) // KT
        acc = lax.fori_loop(start, (lo + QT - 1) // KT + 1, own, acc)
        dq_all[rows, :] = transposed(acc * scale).astype(dq_all.dtype)
        return carry

    lax.fori_loop(0, q_ref.shape[0] // QT, one_tile, 0)
    rows = piece_refs[0].shape[0]
    for k, piece in enumerate(piece_refs):
        piece[...] = dq_all[lanes((me ^ k) * rows, rows), :]


def backward(meta, ends, kh, kf, kt, vh, vf, q, g, stats, rows, *wait):
    total, width = q.shape
    pieces = total // rows
    return pl.pallas_call(
        functools.partial(backward_kernel, 1.0 / math.sqrt(width), len(wait)),
        out_shape=[jax.ShapeDtypeStruct((rows, width), q.dtype)] * pieces
        + [jax.ShapeDtypeStruct((total, width), jnp.float32)] * 2,
        in_specs=[spec(SMEM)] * 2 + [spec(VMEM)] * 8 + [spec(pl.ANY)] * len(wait),
        out_specs=[spec(VMEM)] * (pieces + 2),
        scratch_shapes=[
            VMEM((total, width), q.dtype),
        ],
        compiler_params=params(),
        cost_estimate=COST(0, 4 << 20),
        name="backward",
    )(meta, ends, kh, kf, kt, vh, vf, q, g, stats, *wait)


def later_kernel(
    scale, waits, meta_ref, ends_ref, kf, vf, qh, gh, dk_in, dv_in, *refs
):
    dv_refs, (dk_ref, dk, dv, stats) = refs[waits:-4], refs[-4:]
    me, base, limit = meta_ref[0], meta_ref[1], meta_ref[2]
    own_rows = kf.shape[0]
    dk[...] = dk_in[...]
    dv[...] = dv_in[...]
    for n in range(qh.shape[0] // STAT_COLS):
        lo = qh.shape[0] + n * STAT_ROWS
        block = gh[lo : lo + STAT_ROWS, :].astype(jnp.float32)
        for row in range(2):
            value = block[3 * row : 3 * row + 1] + block[3 * row + 1 : 3 * row + 2]
            value += block[3 * row + 2 : 3 * row + 3]
            stats[row : row + 1, n * STAT_COLS : (n + 1) * STAT_COLS] = value

    def one_tile(i, carry):
        lo = i * QT
        query_row, first_row, first = query_tile(base + own_rows, lo, ends_ref, base)
        rows = lanes(lo, QT)
        query, grad = qh[rows, :], gh[rows, :]
        lse, delta = stats[0:1, rows], stats[1:2, rows]

        def step(t, carry):
            at = lanes(t * KT, KT)
            mask = allowed(t * KT, query_row, first_row)
            probs, dscores = tile_terms(
                scale, kf[at, :], vf[at, :], query, grad, lse, delta, mask
            )
            dv[at, :] += dot_nn(probs, grad)
            dk[at, :] += dot_nn(dscores, query)
            return carry

        return lax.fori_loop(jnp.minimum(first, own_rows) // KT, own_rows // KT, step, carry)

    tiles = jnp.where(base + own_rows < limit, qh.shape[0] // QT, 0)
    lax.fori_loop(0, tiles, one_tile, 0)
    dk_ref[...] = (dk[...] * scale).astype(dk_ref.dtype)
    rows = dv_refs[0].shape[0]
    for k, piece in enumerate(dv_refs):
        piece[...] = dv[lanes((me ^ k) * rows, rows), :].astype(piece.dtype)


def spread_kernel(waits, me_ref, x_ref, *refs):
    piece_refs = refs[waits:]
    rows = piece_refs[0].shape[0]
    for k, piece in enumerate(piece_refs):
        piece[...] = x_ref[lanes((me_ref[0] ^ k) * rows, rows), :]


def spread(me, x, rows, *wait):
    pieces, width = x.shape[0] // rows, x.shape[1]
    return pl.pallas_call(
        functools.partial(spread_kernel, len(wait)),
        out_shape=[jax.ShapeDtypeStruct((rows, width), x.dtype)] * pieces,
        in_specs=[spec(SMEM), spec(VMEM)] + [spec(pl.ANY)] * len(wait),
        out_specs=[spec(VMEM)] * pieces,
        compiler_params=params(),
        cost_estimate=COST(0, 4 << 20),
        name="spread",
    )(me, x, *wait)


def later(meta, ends, kf, vf, qh, gh, dk, dv, rows, *wait):
    total, width = kf.shape
    pieces = total // rows
    return pl.pallas_call(
        functools.partial(later_kernel, 1.0 / math.sqrt(width), len(wait)),
        out_shape=[jax.ShapeDtypeStruct((rows, width), kf.dtype)] * pieces
        + [jax.ShapeDtypeStruct((total, width), kf.dtype)],
        in_specs=[spec(SMEM)] * 2 + [spec(VMEM)] * 6 + [spec(pl.ANY)] * len(wait),
        out_specs=[spec(VMEM)] * (pieces + 1),
        scratch_shapes=[VMEM((total, width), jnp.float32)] * 2
        + [VMEM((2, qh.shape[0]), jnp.float32)],
        compiler_params=params(),
        cost_estimate=COST(0, 4 << 20),
        name="later",
    )(meta, ends, kf, vf, qh, gh, dk, dv, *wait)


def place_kernel(me_ref, *refs):
    pieces, whole = refs[:-1], refs[-1]
    for k, piece in enumerate(pieces):
        width = piece.shape[1]
        whole[:, lanes((me_ref[0] ^ k) * width, width)] = piece[...]


def place(me, pieces):
    rows, width = pieces[0].shape
    return pl.pallas_call(
        place_kernel,
        out_shape=jax.ShapeDtypeStruct((rows, len(pieces) * width), pieces[0].dtype),
        in_specs=[spec(SMEM)] + [spec(VMEM)] * len(pieces),
        out_specs=spec(VMEM),
        compiler_params=params(),
        cost_estimate=COST(0, 4 << 20),
        name="place",
    )(me, *pieces)


def finish_kernel(count, me_ref, gates_ref, values_ref, *refs):
    pieces, (grads, dots, mixed, columns, gates) = refs[:count], refs[-5:]
    _, heads, top, width = values_ref.shape
    for k, piece in enumerate(pieces):
        mixed[:, lanes((me_ref[0] ^ k) * width, width)] = piece[...]
    gates[...] = gates_ref[...].T

    def step(i, carry):
        at = lanes(i * STEP, STEP)
        for h in range(heads):
            grad = mixed[at, h * width : (h + 1) * width].astype(jnp.float32)
            for j in range(top):
                col = h * top + j
                grads[at, h, j, :] = (gates[at, col : col + 1] * grad).astype(grads.dtype)
                value = values_ref[at, h, j, :].astype(jnp.float32)
                columns[at, col : col + 1] = jnp.sum(grad * value, axis=1, keepdims=True)
        return carry

    lax.fori_loop(0, mixed.shape[0] // STEP, step, 0)
    dots[...] = columns[...].T


def finish(me, gates, values, pieces, *wait):
    rows, heads, top, width = values.shape
    return pl.pallas_call(
        functools.partial(finish_kernel, len(pieces)),
        out_shape=[
            jax.ShapeDtypeStruct(values.shape, values.dtype),
            jax.ShapeDtypeStruct(gates.shape, jnp.float32),
        ],
        in_specs=[spec(SMEM)] + [spec(VMEM)] * (2 + heads) + [spec(pl.ANY)] * len(wait),
        out_specs=[spec(VMEM)] * 2,
        scratch_shapes=[
            VMEM((rows, heads * width), values.dtype),
            VMEM((rows, heads * top), jnp.float32),
            VMEM((rows, heads * top), jnp.float32),
        ],
        compiler_params=params(),
        cost_estimate=COST(0, 5 * values.size),
        name="finish",
    )(me, gates, values, *pieces, *wait)


def gate_table(expert_logits, expert_index):
    index = jnp.transpose(expert_index, (1, 2, 0))
    experts = jnp.arange(expert_logits.shape[2], dtype=jnp.int32)
    onehot = (index[:, :, None, :] == experts[:, None]).astype(jnp.float32)
    logits = jnp.transpose(expert_logits, (1, 2, 0))
    return jax.nn.sigmoid(jnp.sum(onehot * logits[:, None], axis=2)), index


def run(swap, queries, keys, value_sel, expert_logits, expert_index, doc_lengths, grad_attended):
    rows = queries.shape[0]
    heads, top, width = value_sel.shape[1:]
    blocks = lax.axis_size("seq")
    groups = lax.axis_size("dp")
    block = lax.axis_index("seq")
    me = lax.rem(block, heads)
    base = (block - me) * rows
    meta = jnp.stack([me, base, blocks * rows]).astype(jnp.int32)
    ends = jnp.cumsum(doc_lengths[0]).astype(jnp.int32)

    def partner(i, k):
        return i - i % heads + (i % heads ^ k)

    def send(x, k):
        return lax.ppermute(x, "seq", [(i, partner(i, k)) for i in range(blocks)])

    def send_back(x, k):
        if not swap:
            return send(x, k) if k else x
        route = [
            (g * blocks + i, (groups - 1 - g) * blocks + partner(i, k))
            for g in range(groups)
            for i in range(blocks)
        ]
        return lax.ppermute(x, ("dp", "seq"), route)

    def exchange(pieces):
        return [pieces[0]] + [send(pieces[k], k) for k in range(1, heads)]

    def shift(x, by):
        route = [(i, i + by) for i in range(blocks) if 0 <= i + by < blocks]
        return lax.ppermute(x, "seq", route)

    gates, index = gate_table(expert_logits, expert_index)
    gates = gates.reshape(heads * top, rows)
    if swap:
        other = [(g, groups - 1 - g) for g in range(groups)]
        table = jnp.concatenate([gates, index.reshape(heads * top, rows).astype(jnp.float32)])
        table = lax.ppermute(table, "dp", other)
        final_gates, final_index = table[: heads * top], table[heads * top :].astype(jnp.int32)
        final_values = lax.ppermute(value_sel, "dp", other)
        early = (final_gates, final_values)
    else:
        final_gates, final_index, final_values = gates, index, value_sel
        early = ()

    key_packed = pack(meta, keys, heads)
    key_pieces = exchange(key_packed)
    value_packed = mix(meta, gates, value_sel, key_packed[0])
    value_pieces = exchange(value_packed)
    kf, k_up = order(meta, key_pieces, [heads - HALO], value_packed[0])
    kh = shift(k_up, heads)
    query_packed = pack(meta, queries, heads, kf, *early)
    query_pieces = exchange(query_packed)
    vf, v_up = order(meta, value_pieces, [heads - HALO], query_packed[0])
    vh = shift(v_up, heads)
    grad_packed = pack(meta, grad_attended, heads, vf)
    grad_pieces = exchange(grad_packed)
    qf, q_down = order(meta, query_pieces, [0], grad_packed[0])
    qh = shift(q_down, -heads)
    near_out, near_lse, kt = near(meta, ends, kf, vf, qf, qf)
    (gf,) = order(meta, grad_pieces, [None], near_lse)

    *out, stats, down = reach(meta, ends, kh, vh, qf, gf, near_out, near_lse, rows)
    gh = shift(down, -heads)
    out_got = [send_back(out[k], k) for k in range(1, heads)]
    *dq, dk, dv = backward(meta, ends, kh, kf, kt, vh, vf, qf, gf, stats, rows, qh)
    dq_got = [send_back(dq[k], k) for k in range(1, heads)]
    *dv, dk = later(meta, ends, kf, vf, qh, gh, dk, dv, rows, *out_got)
    dv_got = [send_back(dv[k], k) for k in range(1, heads)]
    dk = spread(meta, dk, rows, *dq_got)
    dk_got = [send_back(dk[k], k) for k in range(1, heads)]
    own = [out[0], dq[0], dv[0], dk[0]]
    if swap:
        own = list(lax.ppermute(jnp.stack(own), "dp", other))
    attended = place(meta, own[:1] + out_got)
    grad_queries = place(meta, own[1:2] + dq_got)
    grad_values, gate_grad = finish(
        meta, final_gates, final_values, own[2:3] + dv_got, attended, grad_queries
    )
    chosen_grad = (gate_grad * final_gates * (1.0 - final_gates)).reshape(heads, top, 1, rows)
    final_index = final_index.reshape(heads, top, 1, rows)
    experts = jnp.arange(expert_logits.shape[2], dtype=jnp.int32)
    onehot = (final_index == experts[:, None]).astype(jnp.float32)
    router_logit_gradient = jnp.transpose(jnp.sum(onehot * chosen_grad, axis=1), (2, 0, 1))
    return attended, grad_queries, place(meta, own[3:] + dk_got), grad_values, router_logit_gradient


def shards(
    queries, keys, value_sel, expert_logits, expert_index, doc_lengths, group_plan, grad_attended
):
    operands = (
        queries,
        keys,
        value_sel,
        expert_logits,
        expert_index,
        doc_lengths,
        grad_attended,
    )
    return lax.cond(
        group_plan[0] == 0,
        functools.partial(run, False),
        functools.partial(run, True),
        *operands,
    )


def solution(mesh):
    in_specs = (
        P(("dp", "seq"), None),
        P(("dp", "seq"), None),
        P(("dp", "seq"), None, None, None),
        P(("dp", "seq"), None, None),
        P(("dp", "seq"), None, None),
        P("dp", None),
        P(),
        P(("dp", "seq"), None),
    )
    out_specs = (
        P(("dp", "seq"), None),
        P(("dp", "seq"), None),
        P(("dp", "seq"), None),
        P(("dp", "seq"), None, None, None),
        P(("dp", "seq"), None, None),
    )
    return jax.shard_map(shards, mesh=mesh, in_specs=in_specs, out_specs=out_specs, check_vma=False)
```

```python
import functools
import math

import jax
import jax.numpy as jnp
from jax import lax
from jax.experimental import pallas as pl
from jax.experimental.pallas import tpu as pltpu
from jax.sharding import PartitionSpec as P

HALO = 3
NEG = -1e30
QT = 512
KT = 512
VMEM = pltpu.VMEM
SMEM = pltpu.SMEM
LOG2E = math.log2(math.e)
STEP = 64
STAT_ROWS = 16
STAT_COLS = 256


def COST(flops, size):
    return pl.CostEstimate(flops=0, bytes_accessed=1, transcendentals=0)


def spec(space):
    return pl.BlockSpec(memory_space=space)


def params(mib=48):
    return pltpu.CompilerParams(vmem_limit_bytes=mib * 1024 * 1024)


def pick(me, x, k, width):
    return x[:, pl.ds(pl.multiple_of((me ^ k) * width, width), width)]


def pack_kernel(waits, me_ref, x_ref, *refs):
    for k, piece in enumerate(refs[waits:]):
        piece[...] = pick(me_ref[0], x_ref, k, piece.shape[1])


def pack(me, x, heads, *wait):
    rows, width = x.shape[0], x.shape[1] // heads
    return pl.pallas_call(
        functools.partial(pack_kernel, len(wait)),
        out_shape=[jax.ShapeDtypeStruct((rows, width), x.dtype)] * heads,
        in_specs=[spec(SMEM), spec(VMEM)] + [spec(pl.ANY)] * len(wait),
        out_specs=[spec(VMEM)] * heads,
        compiler_params=params(),
        cost_estimate=COST(0, 4 * x.size),
        name="pack",
    )(me, x, *wait)


def stack_kernel(x_ref, *refs):
    out_ref = refs[-1]
    width = out_ref.shape[2]
    for h in range(out_ref.shape[0]):
        out_ref[h] = x_ref[:, h * width : (h + 1) * width]


def stack_heads(x, heads, *wait):
    rows, width = x.shape[0], x.shape[1] // heads
    return pl.pallas_call(
        stack_kernel,
        out_shape=jax.ShapeDtypeStruct((heads, rows, width), x.dtype),
        in_specs=[spec(VMEM)] + [spec(pl.ANY)] * len(wait),
        out_specs=spec(VMEM),
        compiler_params=params(),
        cost_estimate=COST(0, 4 * x.size),
        name="stack",
    )(x, *wait)


def mix_kernel(waits, me_ref, gates_ref, values_ref, *refs):
    piece_refs, (mixed, columns) = refs[waits:-2], refs[-2:]
    _, heads, top, width = values_ref.shape
    columns[...] = gates_ref[...].T

    def step(i, carry):
        at = lanes(i * STEP, STEP)
        for h in range(heads):
            total = 0.0
            for j in range(top):
                col = h * top + j
                gate = columns[at, col : col + 1]
                total += gate * values_ref[at, h, j, :].astype(jnp.float32)
            mixed[at, h * width : (h + 1) * width] = total.astype(mixed.dtype)
        return carry

    lax.fori_loop(0, mixed.shape[0] // STEP, step, 0)
    for k, piece in enumerate(piece_refs):
        piece[...] = pick(me_ref[0], mixed, k, width)


def mix(me, gates, values, *wait):
    rows, heads, _, width = values.shape
    return pl.pallas_call(
        functools.partial(mix_kernel, len(wait)),
        out_shape=[jax.ShapeDtypeStruct((rows, width), values.dtype)] * heads,
        in_specs=[spec(SMEM)] + [spec(VMEM)] * 2 + [spec(pl.ANY)] * len(wait),
        out_specs=[spec(VMEM)] * heads,
        scratch_shapes=[
            VMEM((rows, heads * width), values.dtype),
            VMEM(gates.shape[::-1], jnp.float32),
        ],
        compiler_params=params(),
        cost_estimate=COST(0, 3 * values.size),
        name="mix",
    )(me, gates, values, *wait)


def order_kernel(skips, count, waits, me_ref, *refs):
    pieces, outs = refs[:count], list(refs[count + waits :])
    rows = pieces[0].shape[0] // len(skips)
    for n, skip in enumerate(skips):
        whole = outs.pop(0)
        part = None if skip is None else outs.pop(0)
        for k, piece in enumerate(pieces):
            place = me_ref[0] ^ k
            value = piece[n * rows : (n + 1) * rows, :]
            whole[lanes(place * rows, rows), :] = value
            if part is None:
                continue
            kept = place - skip

            @pl.when((kept >= 0) & (kept < part.shape[0] // rows))
            def _(part=part, kept=kept, value=value):
                part[lanes(kept * rows, rows), :] = value


def order(me, pieces, skips, *wait):
    rows, width = pieces[0].shape[0] // len(skips), pieces[0].shape[1]
    shapes = []
    for skip in skips:
        shapes.append((len(pieces) * rows, width))
        if skip is not None:
            shapes.append((HALO * rows, width))
    return pl.pallas_call(
        functools.partial(order_kernel, skips, len(pieces), len(wait)),
        out_shape=[jax.ShapeDtypeStruct(shape, pieces[0].dtype) for shape in shapes],
        in_specs=[spec(SMEM)] + [spec(VMEM)] * len(pieces) + [spec(pl.ANY)] * len(wait),
        out_specs=[spec(VMEM)] * len(shapes),
        compiler_params=params(),
        cost_estimate=COST(0, 12 * rows * width),
        name="order",
    )(me, *pieces, *wait)


def first_key(position, ends_ref):
    found = jnp.zeros_like(position)
    for n in range(ends_ref.shape[0]):
        found = jnp.where(ends_ref[n] <= position, ends_ref[n], found)
    return found


def dot_nt(a, b):
    return lax.dot_general(a, b, (((1,), (1,)), ((), ())), preferred_element_type=jnp.float32)


def dot_nn(a, b):
    return lax.dot_general(a, b, (((1,), (0,)), ((), ())), preferred_element_type=jnp.float32)


def lanes(start, size):
    return pl.ds(pl.multiple_of(start, size), size)


def transposed(x):
    return x.T


def fill_transposed(dst, src):
    def step(i, carry):
        at = lanes(i * KT, KT)
        dst[:, at] = transposed(src[at, :])
        return carry

    lax.fori_loop(0, src.shape[0] // KT, step, 0)


def query_tile(base, lo, ends_ref, origin):
    pos = base + lo + lax.broadcasted_iota(jnp.int32, (1, QT), 1)
    start = jnp.zeros((), jnp.int32) + base + lo
    return pos - origin, first_key(pos, ends_ref) - origin, first_key(start, ends_ref) - origin


def allowed(key_lo, query_row, first_row):
    key = lax.broadcasted_iota(jnp.int32, (KT, QT), 0)
    return (key >= first_row - key_lo) & (key <= query_row - key_lo)


def online_step(scale, key, value_t, query, mask, state):
    top, total, acc = state
    scores = jnp.where(mask, dot_nt(key, query) * (scale * LOG2E), NEG)
    new_top = jnp.maximum(top, jnp.max(scores, axis=0, keepdims=True))
    expo = jnp.exp2(scores - new_top)
    fade = jnp.exp2(top - new_top)
    total = total * fade + jnp.sum(expo, axis=0, keepdims=True)
    acc = acc * fade + dot_nn(value_t, expo.astype(jnp.bfloat16))
    return new_top, total, acc


def near_kernel(scale, meta_ref, ends_ref, kf, vf, q_ref, wait, out_ref, lse_ref, k_t, v_t):
    del wait
    base = meta_ref[1]
    width = q_ref.shape[1]
    fill_transposed(v_t, vf)
    fill_transposed(k_t, kf)

    def one_tile(i, carry):
        lo = i * QT
        query_row, first_row, first = query_tile(base, lo, ends_ref, base)
        rows = lanes(lo, QT)
        query = q_ref[rows, :]

        def step(t, state):
            at = lanes(t * KT, KT)
            mask = allowed(t * KT, query_row, first_row)
            return online_step(scale, kf[at, :], v_t[:, at], query, mask, state)

        state = (
            jnp.full((1, QT), NEG, jnp.float32),
            jnp.zeros((1, QT), jnp.float32),
            jnp.zeros((width, QT), jnp.float32),
        )
        last = (lo + QT - 1) // KT + 1
        top, total, acc = lax.fori_loop(jnp.maximum(first, 0) // KT, last, step, state)
        out_ref[rows, :] = transposed(acc * (1.0 / total))
        lse_ref[0:1, rows] = top + jnp.log2(total)
        return carry

    lax.fori_loop(0, q_ref.shape[0] // QT, one_tile, 0)


def near(meta, ends, kf, vf, q, wait):
    total, width = q.shape
    return pl.pallas_call(
        functools.partial(near_kernel, 1.0 / math.sqrt(width)),
        out_shape=[
            jax.ShapeDtypeStruct((total, width), jnp.float32),
            jax.ShapeDtypeStruct((1, total), jnp.float32),
            jax.ShapeDtypeStruct((width, total), kf.dtype),
        ],
        in_specs=[spec(SMEM)] * 2 + [spec(VMEM)] * 3 + [spec(pl.ANY)],
        out_specs=[spec(VMEM)] * 3,
        scratch_shapes=[VMEM((width, total), q.dtype)],
        compiler_params=params(),
        cost_estimate=COST(0, 4 << 20),
        name="near",
    )(meta, ends, kf, vf, q, wait)


def reach_kernel(
    scale, meta_ref, ends_ref, kh, vh, q_ref, g_ref, near_ref, near_lse, *refs
):
    piece_refs, (stats, down, out_all) = refs[:-3], refs[-3:]
    me, base = meta_ref[0], meta_ref[1]
    halo_rows = kh.shape[0]
    origin = base - halo_rows

    def one_tile(i, carry):
        lo = i * QT
        query_row, first_row, first = query_tile(base, lo, ends_ref, origin)
        rows = lanes(lo, QT)

        @pl.when(first >= halo_rows)
        def _():
            out_all[rows, :] = near_ref[rows, :]
            stats[0:1, rows] = near_lse[0:1, rows]

        @pl.when(first < halo_rows)
        def _():
            query = q_ref[rows, :]

            def step(t, state):
                at = lanes(t * KT, KT)
                mask = allowed(t * KT, query_row, first_row)
                return online_step(
                    scale, kh[at, :], transposed(vh[at, :]), query, mask, state
                )

            state = (
                near_lse[0:1, rows],
                jnp.ones((1, QT), jnp.float32),
                transposed(near_ref[rows, :]),
            )
            top, total, acc = lax.fori_loop(first // KT, halo_rows // KT, step, state)
            out_all[rows, :] = transposed(acc * (1.0 / total))
            stats[0:1, rows] = top + jnp.log2(total)

        product = g_ref[rows, :].astype(jnp.float32) * out_all[rows, :]
        stats[1:2, rows] = jnp.sum(transposed(product), axis=0, keepdims=True)
        return carry

    lax.fori_loop(0, q_ref.shape[0] // QT, one_tile, 0)
    rows = piece_refs[0].shape[0]
    for k, piece in enumerate(piece_refs):
        piece[...] = out_all[lanes((me ^ k) * rows, rows), :].astype(piece.dtype)
    down[:halo_rows, :] = g_ref[:halo_rows, :]
    for n in range(halo_rows // STAT_COLS):
        block = []
        for row in range(2):
            left = stats[row : row + 1, n * STAT_COLS : (n + 1) * STAT_COLS]
            for _ in range(3):
                part = left.astype(down.dtype).astype(jnp.float32)
                block.append(part)
                left = left - part
        block.append(jnp.zeros((STAT_ROWS - len(block), STAT_COLS), jnp.float32))
        lo = halo_rows + n * STAT_ROWS
        down[lo : lo + STAT_ROWS, :] = jnp.concatenate(block, axis=0).astype(down.dtype)


def reach(meta, ends, kh, vh, q, g, near_out, near_lse, rows):
    total, width = q.shape
    pieces = total // rows
    down = HALO * rows + HALO * rows // STAT_COLS * STAT_ROWS
    return pl.pallas_call(
        functools.partial(reach_kernel, 1.0 / math.sqrt(width)),
        out_shape=[jax.ShapeDtypeStruct((rows, width), q.dtype)] * pieces
        + [jax.ShapeDtypeStruct((2, total), jnp.float32), jax.ShapeDtypeStruct((down, width), g.dtype)],
        in_specs=[spec(SMEM)] * 2 + [spec(VMEM)] * 6,
        out_specs=[spec(VMEM)] * (pieces + 2),
        scratch_shapes=[VMEM((total, width), jnp.float32)],
        compiler_params=params(),
        cost_estimate=COST(0, 4 << 20),
        name="reach",
    )(meta, ends, kh, vh, q, g, near_out, near_lse)


def tile_terms(scale, key, value, query, grad, lse, delta, mask):
    scores = dot_nt(key, query) * (scale * LOG2E) - lse
    probs = jnp.exp2(jnp.where(mask, scores, NEG))
    dprobs = dot_nt(value, grad)
    return probs.astype(jnp.bfloat16), (probs * (dprobs - delta)).astype(jnp.bfloat16)


def backward_kernel(
    scale, waits, meta_ref, ends_ref, kh, kf, k_t, vh, vf, q_ref, g_ref, stats, *refs
):
    piece_refs = refs[waits:-3]
    dk_ref, dv_ref, dq_all = refs[-3:]
    me, base = meta_ref[0], meta_ref[1]
    width = q_ref.shape[1]
    halo_rows = kh.shape[0]
    origin = base - halo_rows
    dk_ref[...] = jnp.zeros_like(dk_ref)
    dv_ref[...] = jnp.zeros_like(dv_ref)

    def one_tile(i, carry):
        lo = i * QT
        query_row, first_row, first = query_tile(base, lo, ends_ref, origin)
        rows = lanes(lo, QT)
        query, grad = q_ref[rows, :], g_ref[rows, :]
        lse, delta = stats[0:1, rows], stats[1:2, rows]

        def far(t, acc):
            at = lanes(t * KT, KT)
            mask = allowed(t * KT, query_row, first_row)
            key = kh[at, :]
            _, dscores = tile_terms(scale, key, vh[at, :], query, grad, lse, delta, mask)
            return acc + dot_nn(transposed(key), dscores)

        def own(t, acc):
            at = lanes(t * KT, KT)
            mask = allowed(t * KT + halo_rows, query_row, first_row)
            probs, dscores = tile_terms(
                scale, kf[at, :], vf[at, :], query, grad, lse, delta, mask
            )
            dv_ref[at, :] += dot_nn(probs, grad)
            dk_ref[at, :] += dot_nn(dscores, query)
            return acc + dot_nn(k_t[:, at], dscores)

        acc = jnp.zeros((width, QT), jnp.float32)
        acc = lax.fori_loop(first // KT, halo_rows // KT, far, acc)
        start = jnp.maximum(first - halo_rows, 0) // KT
        acc = lax.fori_loop(start, (lo + QT - 1) // KT + 1, own, acc)
        dq_all[rows, :] = transposed(acc * scale).astype(dq_all.dtype)
        return carry

    lax.fori_loop(0, q_ref.shape[0] // QT, one_tile, 0)
    rows = piece_refs[0].shape[0]
    for k, piece in enumerate(piece_refs):
        piece[...] = dq_all[lanes((me ^ k) * rows, rows), :]


def backward(meta, ends, kh, kf, kt, vh, vf, q, g, stats, rows, *wait):
    total, width = q.shape
    pieces = total // rows
    return pl.pallas_call(
        functools.partial(backward_kernel, 1.0 / math.sqrt(width), len(wait)),
        out_shape=[jax.ShapeDtypeStruct((rows, width), q.dtype)] * pieces
        + [jax.ShapeDtypeStruct((total, width), jnp.float32)] * 2,
        in_specs=[spec(SMEM)] * 2 + [spec(VMEM)] * 8 + [spec(pl.ANY)] * len(wait),
        out_specs=[spec(VMEM)] * (pieces + 2),
        scratch_shapes=[
            VMEM((total, width), q.dtype),
        ],
        compiler_params=params(),
        cost_estimate=COST(0, 4 << 20),
        name="backward",
    )(meta, ends, kh, kf, kt, vh, vf, q, g, stats, *wait)


def later_kernel(
    scale, waits, meta_ref, ends_ref, kf, vf, qh, gh, dk_in, dv_in, *refs
):
    dv_refs, (dk_first, dk_ref, dk, dv, stats) = refs[waits:-5], refs[-5:]
    me, base, limit = meta_ref[0], meta_ref[1], meta_ref[2]
    own_rows = kf.shape[0]
    dk[...] = dk_in[...]
    dv[...] = dv_in[...]
    for n in range(qh.shape[0] // STAT_COLS):
        lo = qh.shape[0] + n * STAT_ROWS
        block = gh[lo : lo + STAT_ROWS, :].astype(jnp.float32)
        for row in range(2):
            value = block[3 * row : 3 * row + 1] + block[3 * row + 1 : 3 * row + 2]
            value += block[3 * row + 2 : 3 * row + 3]
            stats[row : row + 1, n * STAT_COLS : (n + 1) * STAT_COLS] = value

    def one_tile(i, carry):
        lo = i * QT
        query_row, first_row, first = query_tile(base + own_rows, lo, ends_ref, base)
        rows = lanes(lo, QT)
        query, grad = qh[rows, :], gh[rows, :]
        lse, delta = stats[0:1, rows], stats[1:2, rows]

        def step(t, carry):
            at = lanes(t * KT, KT)
            mask = allowed(t * KT, query_row, first_row)
            probs, dscores = tile_terms(
                scale, kf[at, :], vf[at, :], query, grad, lse, delta, mask
            )
            dv[at, :] += dot_nn(probs, grad)
            dk[at, :] += dot_nn(dscores, query)
            return carry

        return lax.fori_loop(jnp.minimum(first, own_rows) // KT, own_rows // KT, step, carry)

    tiles = jnp.where(base + own_rows < limit, qh.shape[0] // QT, 0)
    lax.fori_loop(0, tiles, one_tile, 0)
    dk_ref[...] = (dk[...] * scale).astype(dk_ref.dtype)
    rows = dv_refs[0].shape[0]
    dk_first[...] = dk_ref[lanes(me * rows, rows), :]
    for k, piece in enumerate(dv_refs):
        piece[...] = dv[lanes((me ^ k) * rows, rows), :].astype(piece.dtype)


def spread_kernel(waits, me_ref, x_ref, *refs):
    piece_refs = refs[waits:]
    rows = piece_refs[0].shape[0]
    for k, piece in enumerate(piece_refs):
        piece[...] = x_ref[lanes((me_ref[0] ^ k) * rows, rows), :]


def spread(me, x, rows, *wait):
    pieces, width = x.shape[0] // rows, x.shape[1]
    return pl.pallas_call(
        functools.partial(spread_kernel, len(wait)),
        out_shape=[jax.ShapeDtypeStruct((rows, width), x.dtype)] * pieces,
        in_specs=[spec(SMEM), spec(VMEM)] + [spec(pl.ANY)] * len(wait),
        out_specs=[spec(VMEM)] * pieces,
        compiler_params=params(),
        cost_estimate=COST(0, 4 << 20),
        name="spread",
    )(me, x, *wait)


def later(meta, ends, kf, vf, qh, gh, dk, dv, rows, *wait):
    total, width = kf.shape
    pieces = total // rows
    return pl.pallas_call(
        functools.partial(later_kernel, 1.0 / math.sqrt(width), len(wait)),
        out_shape=[jax.ShapeDtypeStruct((rows, width), kf.dtype)] * (pieces + 1)
        + [jax.ShapeDtypeStruct((total, width), kf.dtype)],
        in_specs=[spec(SMEM)] * 2 + [spec(VMEM)] * 6 + [spec(pl.ANY)] * len(wait),
        out_specs=[spec(VMEM)] * (pieces + 2),
        scratch_shapes=[VMEM((total, width), jnp.float32)] * 2
        + [VMEM((2, qh.shape[0]), jnp.float32)],
        compiler_params=params(),
        cost_estimate=COST(0, 4 << 20),
        name="later",
    )(meta, ends, kf, vf, qh, gh, dk, dv, *wait)


def place_kernel(me_ref, *refs):
    pieces, whole = refs[:-1], refs[-1]
    for k, piece in enumerate(pieces):
        width = piece.shape[1]
        whole[:, lanes((me_ref[0] ^ k) * width, width)] = piece[...]


def place(me, pieces):
    rows, width = pieces[0].shape
    return pl.pallas_call(
        place_kernel,
        out_shape=jax.ShapeDtypeStruct((rows, len(pieces) * width), pieces[0].dtype),
        in_specs=[spec(SMEM)] + [spec(VMEM)] * len(pieces),
        out_specs=spec(VMEM),
        compiler_params=params(),
        cost_estimate=COST(0, 4 << 20),
        name="place",
    )(me, *pieces)


def finish_kernel(count, me_ref, gates_ref, values_ref, *refs):
    pieces, (grads, dots, mixed, columns, gates) = refs[:count], refs[-5:]
    _, heads, top, width = values_ref.shape
    for k, piece in enumerate(pieces):
        mixed[:, lanes((me_ref[0] ^ k) * width, width)] = piece[...]
    gates[...] = gates_ref[...].T

    def step(i, carry):
        at = lanes(i * STEP, STEP)
        for h in range(heads):
            grad = mixed[at, h * width : (h + 1) * width].astype(jnp.float32)
            for j in range(top):
                col = h * top + j
                grads[at, h, j, :] = (gates[at, col : col + 1] * grad).astype(grads.dtype)
                value = values_ref[at, h, j, :].astype(jnp.float32)
                columns[at, col : col + 1] = jnp.sum(grad * value, axis=1, keepdims=True)
        return carry

    lax.fori_loop(0, mixed.shape[0] // STEP, step, 0)
    dots[...] = columns[...].T


def finish(me, gates, values, pieces, *wait):
    rows, heads, top, width = values.shape
    return pl.pallas_call(
        functools.partial(finish_kernel, len(pieces)),
        out_shape=[
            jax.ShapeDtypeStruct(values.shape, values.dtype),
            jax.ShapeDtypeStruct(gates.shape, jnp.float32),
        ],
        in_specs=[spec(SMEM)] + [spec(VMEM)] * (2 + heads) + [spec(pl.ANY)] * len(wait),
        out_specs=[spec(VMEM)] * 2,
        scratch_shapes=[
            VMEM((rows, heads * width), values.dtype),
            VMEM((rows, heads * top), jnp.float32),
            VMEM((rows, heads * top), jnp.float32),
        ],
        compiler_params=params(),
        cost_estimate=COST(0, 5 * values.size),
        name="finish",
    )(me, gates, values, *pieces, *wait)


def gate_table(expert_logits, expert_index):
    index = jnp.transpose(expert_index, (1, 2, 0))
    experts = jnp.arange(expert_logits.shape[2], dtype=jnp.int32)
    onehot = (index[:, :, None, :] == experts[:, None]).astype(jnp.float32)
    logits = jnp.transpose(expert_logits, (1, 2, 0))
    return jax.nn.sigmoid(jnp.sum(onehot * logits[:, None], axis=2)), index


def run_stay(queries, keys, value_sel, expert_logits, expert_index, doc_lengths, grad_attended):
    rows = queries.shape[0]
    heads, top, width = value_sel.shape[1:]
    blocks = lax.axis_size("seq")
    groups = lax.axis_size("dp")
    block = lax.axis_index("seq")
    me = lax.rem(block, heads)
    base = (block - me) * rows
    meta = jnp.stack([me, base, blocks * rows]).astype(jnp.int32)
    ends = jnp.cumsum(doc_lengths[0]).astype(jnp.int32)

    def partner(i, k):
        return i - i % heads + (i % heads ^ k)

    def send(x, k):
        return lax.ppermute(x, "seq", [(i, partner(i, k)) for i in range(blocks)])

    def exchange(pieces):
        return [pieces[0]] + [send(pieces[k], k) for k in range(1, heads)]

    def shift(x, by):
        route = [(i, i + by) for i in range(blocks) if 0 <= i + by < blocks]
        return lax.ppermute(x, "seq", route)

    gates, index = gate_table(expert_logits, expert_index)
    gates = gates.reshape(heads * top, rows)
    key_packed = pack(meta, keys, heads)
    key_pieces = exchange(key_packed)
    value_packed = mix(meta, gates, value_sel, key_packed[0])
    value_pieces = exchange(value_packed)
    runs = [list(range(lo, lo + heads)) for lo in range(0, blocks, heads)]
    query_packed = stack_heads(queries, heads, value_packed[0])
    qf = lax.all_to_all(query_packed, "seq", 0, 0, axis_index_groups=runs, tiled=True)
    qf = qf.reshape(heads * rows, width)
    kf, k_up = order(meta, key_pieces, [heads - HALO], query_packed)
    kh = shift(k_up, heads)
    grad_packed = pack(meta, grad_attended, heads, kf)
    grad_pieces = exchange(grad_packed)
    vf, v_up = order(meta, value_pieces, [heads - HALO], grad_packed[0])
    vh = shift(v_up, heads)
    qh = shift(qf[: HALO * rows], -heads)
    near_out, near_lse, kt = near(meta, ends, kf, vf, qf, kh)
    (gf,) = order(meta, grad_pieces, [None], near_lse)

    *out, stats, down = reach(meta, ends, kh, vh, qf, gf, near_out, near_lse, rows)
    gh = shift(down, -heads)
    out_got = [send(out[k], k) for k in range(1, heads)]
    *dq, dk, dv = backward(meta, ends, kh, kf, kt, vh, vf, qf, gf, stats, rows, qh)
    dq_got = [send(dq[k], k) for k in range(1, heads)]
    *dv, dk_own, dk = later(meta, ends, kf, vf, qh, gh, dk, dv, rows, *out_got)
    dv_got = [send(dv[k], k) for k in range(1, heads)]
    own = [out[0], dq[0], dv[0], dk_own]
    dk = spread(meta, dk, rows, *dq_got)
    dk_got = [send(dk[k], k) for k in range(1, heads)]
    attended = place(meta, own[:1] + out_got)
    grad_queries = place(meta, own[1:2] + dq_got)
    grad_values, gate_grad = finish(
        meta, gates, value_sel, own[2:3] + dv_got, attended, grad_queries, dk[0]
    )
    chosen_grad = (gate_grad * gates * (1.0 - gates)).reshape(heads, top, 1, rows)
    experts = jnp.arange(expert_logits.shape[2], dtype=jnp.int32)
    onehot = (index[:, :, None, :] == experts[:, None]).astype(jnp.float32)
    router_logit_gradient = jnp.transpose(jnp.sum(onehot * chosen_grad, axis=1), (2, 0, 1))
    grad_keys = place(meta, own[3:] + dk_got)
    return attended, grad_queries, grad_keys, grad_values, router_logit_gradient


def run_swap(queries, keys, value_sel, expert_logits, expert_index, doc_lengths, grad_attended):
    rows = queries.shape[0]
    heads, top, width = value_sel.shape[1:]
    blocks = lax.axis_size("seq")
    groups = lax.axis_size("dp")
    block = lax.axis_index("seq")
    me = lax.rem(block, heads)
    base = (block - me) * rows
    meta = jnp.stack([me, base, blocks * rows]).astype(jnp.int32)
    ends = jnp.cumsum(doc_lengths[0]).astype(jnp.int32)

    def partner(i, k):
        return i - i % heads + (i % heads ^ k)

    def send(x, k):
        return lax.ppermute(x, "seq", [(i, partner(i, k)) for i in range(blocks)])

    def send_back(x, k):
        route = [
            (g * blocks + i, (groups - 1 - g) * blocks + partner(i, k))
            for g in range(groups)
            for i in range(blocks)
        ]
        return lax.ppermute(x, ("dp", "seq"), route)

    def exchange(pieces):
        return [pieces[0]] + [send(pieces[k], k) for k in range(1, heads)]

    def shift(x, by):
        route = [(i, i + by) for i in range(blocks) if 0 <= i + by < blocks]
        return lax.ppermute(x, "seq", route)

    gates, index = gate_table(expert_logits, expert_index)
    gates = gates.reshape(heads * top, rows)
    other = [(g, groups - 1 - g) for g in range(groups)]
    table = jnp.concatenate([gates, index.reshape(heads * top, rows).astype(jnp.float32)])
    table = lax.ppermute(table, "dp", other)
    final_gates, final_index = table[: heads * top], table[heads * top :].astype(jnp.int32)
    final_values = lax.ppermute(value_sel, "dp", other)

    key_packed = pack(meta, keys, heads)
    key_pieces = exchange(key_packed)
    value_packed = mix(meta, gates, value_sel, key_packed[0])
    value_pieces = exchange(value_packed)
    query_packed = pack(meta, queries, heads, value_packed[0], final_gates, final_values)
    query_pieces = exchange(query_packed)
    kf, k_up = order(meta, key_pieces, [heads - HALO], query_packed[0])
    kh = shift(k_up, heads)
    grad_packed = pack(meta, grad_attended, heads, kf)
    grad_pieces = exchange(grad_packed)
    vf, v_up = order(meta, value_pieces, [heads - HALO], *query_pieces)
    vh = shift(v_up, heads)
    qf, q_down = order(meta, query_pieces, [0], vf)
    qh = shift(q_down, -heads)
    near_out, near_lse, kt = near(meta, ends, kf, vf, qf, kh)
    (gf,) = order(meta, grad_pieces, [None], near_lse)

    *out, stats, down = reach(meta, ends, kh, vh, qf, gf, near_out, near_lse, rows)
    gh = shift(down, -heads)
    out_got = [send_back(out[k], k) for k in range(1, heads)]
    *dq, dk, dv = backward(meta, ends, kh, kf, kt, vh, vf, qf, gf, stats, rows, qh)
    dq_got = [send_back(dq[k], k) for k in range(1, heads)]
    *dv, _, dk = later(meta, ends, kf, vf, qh, gh, dk, dv, rows, *out_got)
    dv_got = [send_back(dv[k], k) for k in range(1, heads)]
    dk = spread(meta, dk, rows, *dq_got)
    dk_got = [send_back(dk[k], k) for k in range(1, heads)]
    own = [out[0], dq[0], dv[0], dk[0]]
    own = list(lax.ppermute(jnp.stack(own), "dp", other))
    attended = place(meta, own[:1] + out_got)
    grad_queries = place(meta, own[1:2] + dq_got)
    grad_values, gate_grad = finish(
        meta, final_gates, final_values, own[2:3] + dv_got, attended, grad_queries
    )
    chosen_grad = (gate_grad * final_gates * (1.0 - final_gates)).reshape(heads, top, 1, rows)
    final_index = final_index.reshape(heads, top, 1, rows)
    experts = jnp.arange(expert_logits.shape[2], dtype=jnp.int32)
    onehot = (final_index == experts[:, None]).astype(jnp.float32)
    router_logit_gradient = jnp.transpose(jnp.sum(onehot * chosen_grad, axis=1), (2, 0, 1))
    return attended, grad_queries, place(meta, own[3:] + dk_got), grad_values, router_logit_gradient


def shards(
    queries, keys, value_sel, expert_logits, expert_index, doc_lengths, group_plan, grad_attended
):
    operands = (
        queries,
        keys,
        value_sel,
        expert_logits,
        expert_index,
        doc_lengths,
        grad_attended,
    )
    return lax.cond(
        group_plan[0] == 0,
        run_stay,
        run_swap,
        *operands,
    )


def solution(mesh):
    in_specs = (
        P(("dp", "seq"), None),
        P(("dp", "seq"), None),
        P(("dp", "seq"), None, None, None),
        P(("dp", "seq"), None, None),
        P(("dp", "seq"), None, None),
        P("dp", None),
        P(),
        P(("dp", "seq"), None),
    )
    out_specs = (
        P(("dp", "seq"), None),
        P(("dp", "seq"), None),
        P(("dp", "seq"), None),
        P(("dp", "seq"), None, None, None),
        P(("dp", "seq"), None, None),
    )
    return jax.shard_map(shards, mesh=mesh, in_specs=in_specs, out_specs=out_specs, check_vma=False)
```
